256 devices in a mesh: req: 32 (over y, x, core), tp: 8 (over z).
Axes of the slice: x: 4, y: 4, z: 8, core: 2. Of those that a mesh axis runs over, the one named last changes fastest.
Arguments:
- queries: bfloat16 [2048, 8192], P('req', 'tp'), may hold values from -120 to 120
- key_cache: bfloat16 [2048, 8, 64, 128], P('req', 'tp'), may hold values from -4.1 to 4.1
- value_cache: bfloat16 [2048, 8, 64, 128], P('req', 'tp'), may hold values from -6 to 6
- new_key: bfloat16 [2048, 1024], P('req', 'tp'), may hold values from -6 to 6
- new_value: bfloat16 [2048, 1024], P('req', 'tp'), may hold values from -6 to 6
- cache_length: int32 [2048], P('req'), may hold values from 1 to 64, 65536 in all
- row_adapter: int32 [2048, 1], P('req'), may hold values from 0 to 63; in each aligned block of 64 rows (0 to 63, 64 to 127, ...) at most 2 rows name the same one
- adapter_home: int32 [64], replicated, may hold values from 0 to 63, each once
- down_pool: bfloat16 [64, 8192, 16], P('req', 'tp'), may hold values from -0.0625 to 0.0625
- up_pool: bfloat16 [64, 16, 4096], P('req', None, 'tp'), may hold values from -1.5 to 1.5
- out_weight: bfloat16 [8192, 4096], P('tp'), may hold values from -0.0625 to 0.0625
Outputs:
- mixed: bfloat16 [2048, 4096], P('req', 'tp')
The draws below stay inside these ranges and needn't reach their ends.
Inputs may be any that keep to these rules, and one draw needn't show every extreme that they name: `row_adapter`: among the 64 rows of one group no adapter is named by more than 2 rows, and some group has 2 rows on one adapter. `adapter_home`: a permutation; slot s is held by index s // 2 of req.
All inputs are finite; a program needn't handle non-finite values. No bound on the sum of `cache_length` on one device may be relied on, other than what follows from the above.
Results may differ from the reference program's by a relative error of at most 0.015.
Values may be sent and summed in bfloat16 or wider, within the bound.
A program may use at most 64 MiB of HBM per device.

```python
import math
import jax
import jax.numpy as jnp
import numpy as np
from jax import lax

HEADS = 64
KV_HEADS = 8
HEAD_DIM = 128
DOUT = 4096
RANK = 16
CAP = 2
ROW_DEV = 64
CACHE = 64
NADAPT = 64
GROUP = 8
ROWS = 2048
N_REQ = 32


def shared_keys(key):
    return jax.random.truncated_normal(key, -4.0, 4.0, (ROWS, KV_HEADS, CACHE, HEAD_DIM), jnp.float32)


def draw_key_cache(key, part):
    keys = shared_keys(key)
    return keys.astype(jnp.bfloat16)


def draw_queries(key, part):
    key = jax.random.fold_in(key, 12)
    values = jax.random.truncated_normal(key, -4.0, 4.0, (ROWS, HEADS, HEAD_DIM), jnp.float32)
    return values.reshape(ROWS, HEADS * HEAD_DIM).astype(jnp.bfloat16)


def block_scale(stream_key, extent, shards, low, high):
    def one(dim, parts):
        heights = jax.random.uniform(jax.random.fold_in(jax.random.fold_in(stream_key, 6), dim), (parts,), jnp.float32, low / len(shards), high / len(shards))
        return jnp.repeat(jnp.exp(heights), extent[dim] // parts).reshape((-1,) + (1,) * (len(extent) - dim - 1))

    factor_of = one(*shards[0])
    for cut in shards[1:]:
        factor_of = factor_of * one(*cut)
    return factor_of


def split_up(number_of, total, most, slope):
    loads = [(1 << 20) // math.isqrt(grade ** slope) + 1 for grade in range(2, number_of + 1)]
    rest, counts = total - most - (number_of - 1), [1] * (number_of - 1)
    while rest > 0:
        free = [i for i in range(number_of - 1) if counts[i] < most]
        mass, remaining = sum([loads[i] for i in free]), rest
        for i in free:
            extra = min(most - counts[i], max(1, remaining * loads[i] // mass), rest)
            counts[i] = counts[i] + extra
            rest = rest - extra
    return np.array([most] + counts)


def ragged_sizes(stream_key, number_of, total, most, skew):
    if number_of == 2:
        one = jax.random.randint(stream_key, (), max(1, total - most), min(most, total - 1) + 1)
        return jnp.stack([one, total - one])
    sizes = jnp.asarray(split_up(number_of, total, most, skew), jnp.int32)
    pairs = (number_of - 1) // 2
    donor, sink = sizes[1:1 + 2 * pairs:2], sizes[2:2 + 2 * pairs:2]
    slack = jnp.minimum(donor - 1, most - sink)
    moved = jax.random.randint(jax.random.fold_in(stream_key, 1), (pairs,), 0, 1 << 20) % (slack + 1)
    sizes = sizes.at[1:1 + 2 * pairs:2].set(donor - moved).at[2:2 + 2 * pairs:2].set(sink + moved)
    return sizes[jax.random.permutation(jax.random.fold_in(stream_key, 2), number_of)]


def shared_out(stream_key, own, number, rows, count, top, reach, slope):
    sequence = jax.random.permutation(stream_key, count)
    packed, ordinary = portions_of(count, rows * top, reach, slope, True), portions_of(count, rows * top, reach, slope, False)
    places = jnp.arange(count)

    def named(lengths, turn):
        used = int((lengths > 0).sum())
        fixed = max(1, used // 4)
        passed = fixed + (places - fixed + turn * (used - fixed)) % max(1, count - fixed)
        return jnp.zeros((count,), jnp.int32).at[sequence[jnp.where(places < fixed, places, passed)]].set(jnp.asarray(lengths, jnp.int32))

    lengths = jnp.where(number % 4 == 0, named(packed, number // 4), named(ordinary, number - number // 4 - 1))
    mixed = jax.random.permutation(jax.random.fold_in(own, 3), count)
    giver, taker = mixed[0:count // 2 * 2:2], mixed[1:count // 2 * 2:2]
    slack = jnp.minimum(lengths[giver] - 1, reach - lengths[taker]) // 2
    slack = jnp.where((giver == sequence[0]) | (taker == sequence[0]) | (lengths[taker] == 0), 0, jnp.maximum(slack, 0))
    passed = jax.random.randint(jax.random.fold_in(own, 4), (count // 2,), 0, 1 << 20) % (slack + 1)
    lengths = lengths.at[giver].add(-passed).at[taker].add(passed)
    items = jnp.searchsorted(jnp.cumsum(lengths), jnp.arange(rows * top), side="right").astype(jnp.int32)
    table = items.reshape(top, rows).T
    table = table[jax.random.permutation(jax.random.fold_in(own, 1), rows)]
    turn = jax.random.randint(jax.random.fold_in(own, 2), (rows, 1), 0, top)
    return jnp.take_along_axis(table, (jnp.arange(top)[None, :] + turn) % top, axis=1)


def portions_of(number_of, total, limit, lean, full):
    loads = [(1 << 20) // math.isqrt(grade ** lean) + 1 for grade in range(1, number_of + 1)]
    largest = limit if full else min(limit, max(-(-total // number_of), total * loads[0] // sum(loads)))
    least = 1 if total - largest >= number_of - 1 else 0
    given, spare = [largest] + [least] * (number_of - 1), total - largest - least * (number_of - 1)
    while spare > 0:
        free = [i for i in range(1, number_of) if given[i] < largest] or [i for i in range(1, number_of) if given[i] < limit]
        mass, left = sum([loads[i] for i in free]), spare
        for i in free:
            more = min(limit - given[i], max(1, left * loads[i] // mass), spare)
            given[i] = given[i] + more
            spare = spare - more
    return np.array(given)


def bell_draw(key, extent, scale, reach, split=(), kind=jnp.bfloat16):
    result = scale * jax.random.normal(key, extent, jnp.float32)
    if split:
        result = result * block_scale(key, extent, split, -0.22, 0.18)
    return jnp.clip(result, -reach, reach).astype(kind)


def setup_inputs(seed: int = 0) -> dict:
    seeds = jax.random.split(jax.random.key(seed), 12)
    queries = draw_queries(jax.random.fold_in(seeds[11], 71), 0)
    key_cache = draw_key_cache(jax.random.fold_in(seeds[11], 71), 0)
    value_cache = bell_draw(seeds[2], (ROWS, KV_HEADS, CACHE, HEAD_DIM), 1.0, 6.0, ((0, 32), (1, 8)))
    new_key = bell_draw(seeds[3], (ROWS, KV_HEADS * HEAD_DIM), 1.0, 6.0, ((0, 32), (1, 8)))
    new_value = bell_draw(seeds[4], (ROWS, KV_HEADS * HEAD_DIM), 1.0, 6.0, ((0, 32), (1, 8)))
    cache_length = ragged_sizes(seeds[5], ROWS, ROWS * CACHE // 2, CACHE, 2).astype(jnp.int32)
    row_adapter_keys = jax.random.split(jax.random.fold_in(seeds[6], 1), ROWS // ROW_DEV)
    row_adapter_turns = jax.random.permutation(jax.random.fold_in(seeds[6], 3), ROWS // ROW_DEV)
    row_adapter = jax.vmap(lambda own, number: shared_out(jax.random.fold_in(seeds[6], 2), own, number, ROW_DEV, NADAPT, 1, CAP, 2))(row_adapter_keys, row_adapter_turns).reshape((ROWS, 1))
    adapter_home = jax.random.permutation(seeds[7], NADAPT).astype(jnp.int32)
    down_pool = bell_draw(seeds[8], (NADAPT, HEADS * HEAD_DIM, RANK), (HEADS * HEAD_DIM) ** -0.5, 0.0625, ((0, 32), (1, 8)))
    up_pool = bell_draw(seeds[9], (NADAPT, RANK, DOUT), RANK ** -0.5, 1.5, ((0, 32), (2, 8)))
    out_weight = bell_draw(seeds[10], (HEADS * HEAD_DIM, DOUT), (HEADS * HEAD_DIM) ** -0.5, 0.0625, ((0, 8),))
    return {"queries": queries, "key_cache": key_cache, "value_cache": value_cache, "new_key": new_key, "new_value": new_value, "cache_length": cache_length, "row_adapter": row_adapter, "adapter_home": adapter_home, "down_pool": down_pool, "up_pool": up_pool, "out_weight": out_weight}


def attend(queries, key_cache, value_cache, new_key, new_value, cache_length):
    count = queries.shape[0]
    kv_local = key_cache.shape[1]
    scale = 1.0 / (HEAD_DIM ** 0.5)
    query = queries.reshape(count, kv_local, GROUP, HEAD_DIM).astype(jnp.float32)
    fresh_key = new_key.reshape(count, kv_local, HEAD_DIM).astype(jnp.float32)
    fresh_value = new_value.reshape(count, kv_local, HEAD_DIM).astype(jnp.float32)
    scores = jnp.einsum("rkgd,rkld->rkgl", query, key_cache.astype(jnp.float32)) * scale
    fresh = jnp.einsum("rkgd,rkd->rkg", query, fresh_key) * scale
    valid = jnp.arange(CACHE, dtype=jnp.int32)[None, :] < cache_length[:, None]
    valid = valid[:, None, None, :]
    scores = jnp.where(valid, scores, -1e30)
    top = jnp.maximum(jnp.max(scores, axis=3), fresh)
    expo = jnp.where(valid, jnp.exp(scores - top[..., None]), 0.0)
    fresh_expo = jnp.exp(fresh - top)
    total = jnp.sum(expo, axis=3) + fresh_expo
    weights = (expo / total[..., None]).astype(jnp.bfloat16)
    fresh_weight = (fresh_expo / total).astype(jnp.bfloat16)
    mixed = jnp.einsum("rkgl,rkld->rkgd", weights.astype(jnp.float32), value_cache.astype(jnp.float32))
    mixed = mixed + fresh_weight.astype(jnp.float32)[..., None] * fresh_value[:, :, None, :]
    return mixed.reshape(count, kv_local * GROUP * HEAD_DIM).astype(jnp.bfloat16)


def reference(queries, key_cache, value_cache, new_key, new_value, cache_length, row_adapter, adapter_home, down_pool, up_pool, out_weight):
    attended = attend(queries, key_cache, value_cache, new_key, new_value, cache_length)
    slot = adapter_home[row_adapter[:, 0]].astype(jnp.int32)
    width = HEADS * HEAD_DIM
    flat_down = jnp.transpose(down_pool, (1, 0, 2)).reshape(width, NADAPT * RANK)
    every_low = jnp.dot(attended, flat_down, preferred_element_type=jnp.float32).reshape(ROWS, NADAPT, RANK)
    select = (slot[:, None] == jnp.arange(NADAPT, dtype=jnp.int32)[None, :]).astype(jnp.float32)
    low = jnp.sum(select[:, :, None] * every_low, axis=1).astype(jnp.bfloat16)

    def apply_up(block):
        low_block, slot_block = block
        factors = up_pool[slot_block].astype(jnp.float32)
        return jnp.einsum("rq,rqd->rd", low_block.astype(jnp.float32), factors).astype(jnp.bfloat16)

    delta = lax.map(apply_up, (low.reshape(N_REQ, ROW_DEV, RANK), slot.reshape(N_REQ, ROW_DEV)))
    delta = delta.reshape(ROWS, DOUT)
    base = jnp.dot(attended, out_weight, preferred_element_type=jnp.float32)
    return (base + delta.astype(jnp.float32)).astype(jnp.bfloat16)
```

```python
import jax
import jax.numpy as jnp
from jax import lax
from jax.experimental import pallas as pl
from jax.experimental.pallas import tpu as pltpu
from jax.sharding import PartitionSpec as P

MESH = pl.DeviceIdType.MESH
HEAD_DIM = 128
GROUP = 8
ROWS = 64
CACHE = 64
RANK = 16
NEG = -1e30
ORDER = (4, 3, -3, 2, -2, 1, -1, 0)


def kernel(
    q_hbm, k_hbm, v_hbm, nk_hbm, nv_hbm, len_hbm, ad_hbm, home_hbm, down_hbm, up_hbm, w_hbm,
    out_ref,
    q, kk, vv, nk, nv, lens, ad, home, gath, w, att, part, low_own, low_all, rs_src, rs_dst,
    in_sem, kv_sem, w_sem, ag_send, ag_recv, low_send, low_recv, rs_send, rs_recv,
):
    req, z = lax.axis_index("req"), lax.axis_index("tp")
    core = req % 2
    x = (req // 2) % 4
    y = req // 8

    a_me = jnp.where(core == 0, x, y)
    b_me = jnp.where(core == 0, y, x)

    def at(yy, xx, cc):
        return ((yy * 4 + xx) * 2 + cc, z)

    def peer_a(d):
        return at((y + core * d) % 4, (x + (1 - core) * d) % 4, core)

    def peer_b(d):
        return at((y + (1 - core) * d) % 4, (x + core * d) % 4, core)

    sibling = at(y, x, 1 - core)

    def bundle(b):
        return (core * 4 + b % 4) * 128

    own_row = bundle(b_me) + a_me * 32

    loads = [
        (len_hbm, lens), (ad_hbm, ad), (home_hbm, home), (q_hbm, q), (nk_hbm, nk), (nv_hbm, nv),
        (down_hbm.at[:, pl.ds(0, 512)], gath.at[0, pl.ds(pl.multiple_of(own_row, 32), 32)]),
        (down_hbm.at[:, pl.ds(512, 512)], gath.at[1, pl.ds(pl.multiple_of(own_row, 32), 32)]),
        (up_hbm, gath.at[2, pl.ds(pl.multiple_of(own_row, 32), 32)]),
    ]
    loads = [pltpu.make_async_copy(s, d, in_sem.at[i]) for i, (s, d) in enumerate(loads)]
    for i in (6, 7, 8, 3, 0, 4, 5, 1, 2):
        loads[i].start()
    kv = []
    for i in range(4):
        rows = pl.ds(1024 * i, 1024)
        kv.append(pltpu.make_async_copy(k_hbm.at[rows], kk.at[rows], kv_sem.at[0, i]))
        kv.append(pltpu.make_async_copy(v_hbm.at[rows], vv.at[rows], kv_sem.at[1, i]))
    for c in kv:
        c.start()
    ws = []
    for n, o in enumerate(ORDER):
        col = pl.multiple_of(((z + o + 8) % 8) * 512, 512)
        ws.append(pltpu.make_async_copy(w_hbm.at[:, pl.ds(col, 512)], w.at[n], w_sem.at[n]))
        ws[-1].start()

    barrier = pltpu.get_barrier_semaphore()
    peers = [peer_a(1), peer_a(3), peer_a(2), peer_b(1), peer_b(3), sibling]
    peers += [(req, (z + d) % 8) for d in range(1, 8)]
    for p in peers:
        pl.semaphore_signal(barrier, inc=1, device_id=p, device_id_type=MESH)
    pl.semaphore_wait(barrier, len(peers))

    started = []

    def ag_copy(chunk, slot, row, rows, device):
        ref = gath.at[chunk, pl.ds(pl.multiple_of(row, 32), rows)]
        copy = pltpu.make_async_remote_copy(
            src_ref=ref, dst_ref=ref, send_sem=ag_send.at[chunk, slot], recv_sem=ag_recv.at[chunk, slot],
            device_id=device, device_id_type=MESH,
        )
        copy.start()
        started.append(copy)
        return copy

    ag = [dict() for _ in range(3)]

    def ag_first(chunk):
        d = ag[chunk]
        d["a"] = [ag_copy(chunk, i, own_row, 32, peer_a(s)) for i, s in enumerate((1, 3, 2))]

    def ag_second(chunk):
        d = ag[chunk]
        for c in d["a"]:
            c.wait_recv()
        row = bundle(b_me)
        d["up"] = ag_copy(chunk, 3, row, 128, peer_b(1))
        d["dn"] = ag_copy(chunk, 4, row, 128, peer_b(3))
        d["s"] = [ag_copy(chunk, 7, row, 128, sibling)]

    def ag_third(chunk):
        d = ag[chunk]
        d["up"].wait_recv()
        below, above = bundle(b_me + 3), bundle(b_me + 1)
        d["f"] = [ag_copy(chunk, 5, below, 64, peer_b(1))]
        d["s"].append(ag_copy(chunk, 8, below, 128, sibling))
        d["dn"].wait_recv()
        d["f"].append(ag_copy(chunk, 6, above + 64, 64, peer_b(3)))
        d["s"].append(ag_copy(chunk, 9, above, 128, sibling))

    def ag_fourth(chunk):
        d = ag[chunk]
        for c in d["f"]:
            c.wait_recv()
        d["s"].append(ag_copy(chunk, 10, bundle(b_me + 2), 128, sibling))

    def ag_last(chunk):
        for c in ag[chunk]["s"]:
            c.wait_recv()

    for chunk in range(3):
        loads[6 + chunk].wait()
        ag_first(chunk)

    scale = 1.0 / HEAD_DIM**0.5
    sub = lax.broadcasted_iota(jnp.int32, (8, 128), 0)
    sub_wide = lax.broadcasted_iota(jnp.int32, (8, 512), 0)
    lane_wide = lax.broadcasted_iota(jnp.int32, (8, 512), 1)
    sub_new = lax.broadcasted_iota(jnp.int32, (8, 16), 0)
    lane_new = lax.broadcasted_iota(jnp.int32, (8, 16), 1)
    contract = (((1,), (1,)), ((), ()))

    def spread(read, base):
        values = jnp.zeros((8, 128), jnp.int32)
        for r in range(8):
            values = jnp.where(sub == r, read(base + r), values)
        return values

    def attend(i):
        kv[2 * i].wait()
        top_rows = pl.ds(16 * i, 16)
        queries = jnp.concatenate([q[top_rows, pl.ds(128 * h, 128)] for h in range(GROUP)], axis=0)
        keys = kk[pl.ds(1024 * i, 1024), :]
        scores = lax.dot_general(queries, keys, contract, preferred_element_type=jnp.float32)
        fresh = lax.dot_general(queries, nk[top_rows, :], contract, preferred_element_type=jnp.float32)
        scores = scores.reshape(8, 2, 8, 1024)
        fresh = fresh.reshape(8, 2, 8, 16)
        kv[2 * i + 1].wait()
        halves = []
        for t in range(2):
            base = 16 * i + 8 * t
            count = spread(lambda r: lens[r], base)[:, :1]
            valid = (lane_wide // CACHE == sub_wide) & (lane_wide % CACHE < count)
            mine = lane_new == sub_new + 8 * t
            s = jnp.where(valid[None], scores[:, t, :, 512 * t : 512 * t + 512] * scale, NEG)
            f = jnp.where(mine[None], fresh[:, t] * scale, NEG)
            top = jnp.maximum(jnp.max(s, axis=2, keepdims=True), jnp.max(f, axis=2, keepdims=True))
            es, ef = jnp.exp(s - top), jnp.exp(f - top)
            total = jnp.sum(es, axis=2, keepdims=True) + jnp.sum(ef, axis=2, keepdims=True)
            inv = 1.0 / total
            ws_ = (es * inv).reshape(64, 512).astype(jnp.bfloat16)
            wf = (ef * inv).reshape(64, 16).astype(jnp.bfloat16)
            o = jnp.dot(ws_, vv[pl.ds(1024 * i + 512 * t, 512), :], preferred_element_type=jnp.float32)
            o = o + jnp.dot(wf, nv[top_rows, :], preferred_element_type=jnp.float32)
            halves.append(o)
        for h in range(GROUP):
            block = jnp.concatenate([o[8 * h : 8 * h + 8] for o in halves], axis=0)
            att[top_rows, pl.ds(128 * h, 128)] = block.astype(jnp.bfloat16)

    def project(n):
        ws[n].wait()
        part[n] = jnp.dot(att[...], w[n], preferred_element_type=jnp.float32)

    rs = {}

    def rs_step(way, step, half):
        n = (0, 1, 3, 5)[step] if way == 0 or step == 0 else (0, 2, 4, 6)[step]
        cols = pl.ds(256 * half, 256)
        value = part[n, :, cols]
        if (way, step - 1, half) in rs:
            rs[way, step - 1, half].wait_recv()
            value = value + rs_dst[way, step - 1, half].astype(jnp.float32)
        rs_src[way, step, half] = value.astype(jnp.bfloat16)
        copy = pltpu.make_async_remote_copy(
            src_ref=rs_src.at[way, step, half], dst_ref=rs_dst.at[way, step, half],
            send_sem=rs_send.at[way, step, half], recv_sem=rs_recv.at[way, step, half],
            device_id=(req, (z + (1 if way == 0 else 7)) % 8), device_id_type=MESH,
        )
        copy.start()
        started.append(copy)
        rs[way, step, half] = copy

    lane_group = lax.broadcasted_iota(jnp.int32, (8, 128), 1) // RANK

    def places(i):
        slot = spread(lambda r: home[ad[r]], 8 * i)
        c, xx, yy = (slot // 2) % 2, (slot // 4) % 4, slot // 16
        place = jnp.where(c == 0, yy * 4 + xx, xx * 4 + yy)
        return (c * 16 + place) * 2 + slot % 2

    for i in (0, 3, 4, 5):
        loads[i].wait()
    attend(0)
    ag_second(0)
    attend(1)
    ag_second(1)
    attend(2)
    ag_second(2)
    attend(3)
    for n in range(0, 1):
        project(n)
    rs_step(0, 0, 0)
    rs_step(1, 0, 1)
    ag_third(0)
    project(1)
    rs_step(0, 1, 1)
    project(2)
    rs_step(1, 1, 0)
    ag_third(1)
    rs_step(0, 1, 0)
    rs_step(1, 1, 1)
    project(3)
    rs_step(0, 2, 1)
    project(4)
    rs_step(1, 2, 0)
    ag_third(2)
    ag_fourth(0)
    rs_step(0, 2, 0)
    rs_step(1, 2, 1)
    project(5)
    project(6)
    rs_step(0, 3, 1)
    rs_step(1, 3, 0)
    rs_step(0, 3, 0)
    rs_step(1, 3, 1)
    ag_fourth(1)
    project(7)

    loads[1].wait()
    loads[2].wait()
    place = [places(i) for i in range(8)]
    ag_last(0)
    inner = lax.dot_general(att[:, pl.ds(0, 512)], gath[0], contract, preferred_element_type=jnp.float32)
    ag_fourth(2)
    ag_last(1)
    inner = inner + lax.dot_general(
        att[:, pl.ds(512, 512)], gath[1], contract, preferred_element_type=jnp.float32
    )
    packed = jnp.zeros((8, 128), jnp.float32)
    for i in range(8):
        one = jnp.zeros((8, 128), jnp.float32)
        for g in range(8):
            hit = lane_group + 8 * g == place[i]
            one = one + jnp.where(hit, inner[8 * i : 8 * i + 8, 128 * g : 128 * g + 128], 0.0)
        for shift in (64, 32, 16):
            one = one + pltpu.roll(one, shift, 1)
        packed = jnp.where(lane_group == i, one, packed)
    low_own[...] = packed
    low_all[z] = packed
    lows = []
    for d in range(1, 8):
        copy = pltpu.make_async_remote_copy(
            src_ref=low_own, dst_ref=low_all.at[z], send_sem=low_send.at[d - 1], recv_sem=low_recv.at[d - 1],
            device_id=(req, (z + d) % 8), device_id_type=MESH,
        )
        copy.start()
        started.append(copy)
        lows.append(copy)
    for copy in lows:
        copy.wait_recv()
    total = low_all[0]
    for j in range(1, 8):
        total = total + low_all[j]
    rows = []
    for i in range(8):
        one = jnp.where(lane_group == i, total, 0.0)
        for shift in (64, 32, 16):
            one = one + pltpu.roll(one, shift, 1)
        rows.append(
            jnp.concatenate([jnp.where(lane_group + 8 * g == place[i], one, 0.0) for g in range(8)], axis=1)
        )
    low = jnp.concatenate(rows, axis=0).astype(jnp.bfloat16)
    ag_last(2)
    delta = jnp.dot(low, gath[2], preferred_element_type=jnp.float32)
    delta = delta.astype(jnp.bfloat16).astype(jnp.float32)
    for half in range(2):
        cols = pl.ds(256 * half, 256)
        value = part[7, :, cols]
        for way in range(2):
            rs[way, 3, half].wait_recv()
            value = value + rs_dst[way, 3, half].astype(jnp.float32)
        value = value + delta[:, 256 * half : 256 * half + 256]
        out_ref[:, cols] = value.astype(jnp.bfloat16)
    for copy in started:
        copy.wait_send()


def per_device(
    queries, key_cache, value_cache, new_key, new_value, cache_length, row_adapter, adapter_home,
    down_pool, up_pool, out_weight,
):
    down = jnp.transpose(down_pool, (0, 2, 1)).reshape(32, 1024)
    up = up_pool.reshape(32, 512)
    keys = key_cache.reshape(4096, 128)
    values = value_cache.reshape(4096, 128)
    named = row_adapter.reshape(64)
    hbm = pl.BlockSpec(memory_space=pltpu.HBM)
    bf16 = jnp.bfloat16
    dma, vmem, smem = pltpu.SemaphoreType.DMA, pltpu.VMEM, pltpu.SMEM
    return pl.pallas_call(
        kernel,
        out_shape=jax.ShapeDtypeStruct((64, 512), bf16),
        in_specs=[hbm] * 11,
        out_specs=pl.BlockSpec(memory_space=pltpu.VMEM),
        scratch_shapes=[
            vmem((64, 1024), bf16),
            vmem((4096, 128), bf16),
            vmem((4096, 128), bf16),
            vmem((64, 128), bf16),
            vmem((64, 128), bf16),
            smem((64,), jnp.int32),
            smem((64,), jnp.int32),
            smem((64,), jnp.int32),
            vmem((3, 1024, 512), bf16),
            vmem((8, 1024, 512), bf16),
            vmem((64, 1024), bf16),
            vmem((8, 64, 512), jnp.float32),
            vmem((8, 128), jnp.float32),
            vmem((8, 8, 128), jnp.float32),
            vmem((2, 4, 2, 64, 256), bf16),
            vmem((2, 4, 2, 64, 256), bf16),
            dma((9,)),
            dma((2, 4)),
            dma((8,)),
            dma((3, 11)),
            dma((3, 11)),
            dma((7,)),
            dma((7,)),
            dma((2, 4, 2)),
            dma((2, 4, 2)),
        ],
        compiler_params=pltpu.CompilerParams(
            collective_id=0, has_side_effects=True, vmem_limit_bytes=60 * 1024 * 1024
        ),
    )(
        queries, keys, values, new_key, new_value, cache_length, named, adapter_home, down, up, out_weight
    )


def solution(mesh):
    return jax.shard_map(
        per_device,
        mesh=mesh,
        in_specs=(
            P("req", "tp"),
            P("req", "tp", None, None),
            P("req", "tp", None, None),
            P("req", "tp"),
            P("req", "tp"),
            P("req"),
            P("req", None),
            P(),
            P("req", "tp", None),
            P("req", None, "tp"),
            P("tp", None),
        ),
        out_specs=P("req", "tp"),
        check_vma=False,
    )
```

```python
import jax
import jax.numpy as jnp
from jax import lax
from jax.experimental import pallas as pl
from jax.experimental.pallas import tpu as pltpu
from jax.sharding import PartitionSpec as P

MESH = pl.DeviceIdType.MESH
HEAD_DIM = 128
GROUP = 8
ROWS = 64
CACHE = 64
RANK = 16
NEG = -1e30


def kernel(
    q_hbm, k_hbm, v_hbm, nk_hbm, nv_hbm, len_hbm, ad_hbm, home_hbm, down_hbm, up_hbm, w_hbm,
    out_ref,
    q, kk, vv, nk, nv, lens, ad, home, pool_d, pool_u, w, att, own, rs_src, rs_dst,
    x_src, x_dst, low_own, low_all, y_src, y_dst,
    in_sem, kv_sem, w_sem, pool_send, pool_recv, x_send, x_recv, y_send, y_recv, low_send, low_recv,
    rs_send, rs_recv,
):
    req, z = lax.axis_index("req"), lax.axis_index("tp")
    core = req % 2
    x = (req // 2) % 4
    y = req // 8

    a_me = jnp.where(core == 0, x, y)
    b_me = jnp.where(core == 0, y, x)

    def at(yy, xx, cc):
        return ((yy % 4 * 4 + xx % 4) * 2 + cc, z)

    def peer_a(d):
        return at(y + core * d, x + (1 - core) * d, core)

    def owner(kind, d):
        return at(y + d, x, 0) if kind == 0 else at(y, x + d, 1)

    def source(kind, d):
        return at(y + (1 - core) * d, x + core * d, kind)

    sibling = at(y, x, 1 - core)
    own_bundle = core * 4 + b_me
    sib_bundle = jnp.where(core == 0, 4 + x, y)
    sib_source = (1 - core) * 4 + b_me

    own_rows = pl.ds(pl.multiple_of(a_me * 32, 32), 32)
    loads = [
        (len_hbm, lens), (ad_hbm, ad), (home_hbm, home), (q_hbm, q), (nk_hbm, nk), (nv_hbm, nv),
        (down_hbm, pool_d.at[own_rows]), (up_hbm, pool_u.at[own_rows]),
    ]
    loads = [pltpu.make_async_copy(s, d, in_sem.at[i]) for i, (s, d) in enumerate(loads)]
    for i in (0, 3, 4):
        loads[i].start()
    kv = []
    for i in range(4):
        rows = pl.ds(1024 * i, 1024)
        kv.append(pltpu.make_async_copy(k_hbm.at[rows], kk.at[rows], kv_sem.at[0, i]))
        kv.append(pltpu.make_async_copy(v_hbm.at[rows], vv.at[rows], kv_sem.at[1, i]))
    for c in kv[:2]:
        c.start()
    for i in (5, 6, 7, 1, 2):
        loads[i].start()
    for c in kv[2:]:
        c.start()
    other = [t + (z <= t).astype(jnp.int32) for t in range(7)]
    ws = []
    for t, block in enumerate(other + [z]):
        col = pl.multiple_of(block * 512, 512)
        ws.append(pltpu.make_async_copy(w_hbm.at[:, pl.ds(col, 512)], w.at[t], w_sem.at[t]))
        ws[-1].start()

    barrier = pltpu.get_barrier_semaphore()
    peers = [sibling]
    for d in range(1, 4):
        for c in range(2):
            peers += [at(y + d, x, c), at(y, x + d, c)]
    peers += [(req, (z + d) % 8) for d in range(1, 8)]
    for p in peers:
        pl.semaphore_signal(barrier, inc=1, device_id=p, device_id_type=MESH)

    started = []

    def send(src, dst, send_sem, recv_sem, device):
        copy = pltpu.make_async_remote_copy(
            src_ref=src, dst_ref=dst, send_sem=send_sem, recv_sem=recv_sem, device_id=device, device_id_type=MESH
        )
        copy.start()
        started.append(copy)
        return copy

    def received(src, dst, recv_sem):
        pltpu.make_async_remote_copy(
            src_ref=src, dst_ref=dst, send_sem=low_send.at[0], recv_sem=recv_sem, device_id=sibling,
            device_id_type=MESH,
        ).wait_recv()

    scale = 1.0 / HEAD_DIM**0.5
    sub = lax.broadcasted_iota(jnp.int32, (8, 128), 0)
    sub_wide = lax.broadcasted_iota(jnp.int32, (8, 512), 0)
    lane_wide = lax.broadcasted_iota(jnp.int32, (8, 512), 1)
    sub_new = lax.broadcasted_iota(jnp.int32, (8, 16), 0)
    lane_new = lax.broadcasted_iota(jnp.int32, (8, 16), 1)
    contract = (((1,), (1,)), ((), ()))

    def spread(read, base):
        values = jnp.zeros((8, 128), jnp.int32)
        for r in range(8):
            values = jnp.where(sub == r, read(base + r), values)
        return values

    def attend(i):
        kv[2 * i].wait()
        top_rows = pl.ds(16 * i, 16)
        queries = jnp.concatenate([q[top_rows, pl.ds(128 * h, 128)] for h in range(GROUP)], axis=0)
        keys = kk[pl.ds(1024 * i, 1024), :]
        scores = lax.dot_general(queries, keys, contract, preferred_element_type=jnp.float32)
        fresh = lax.dot_general(queries, nk[top_rows, :], contract, preferred_element_type=jnp.float32)
        scores = scores.reshape(8, 2, 8, 1024)
        fresh = fresh.reshape(8, 2, 8, 16)
        kv[2 * i + 1].wait()
        halves = []
        for t in range(2):
            base = 16 * i + 8 * t
            count = spread(lambda r: lens[r], base)[:, :1]
            valid = (lane_wide // CACHE == sub_wide) & (lane_wide % CACHE < count)
            mine = lane_new == sub_new + 8 * t
            s = jnp.where(valid[None], scores[:, t, :, 512 * t : 512 * t + 512] * scale, NEG)
            f = jnp.where(mine[None], fresh[:, t] * scale, NEG)
            top = jnp.maximum(jnp.max(s, axis=2, keepdims=True), jnp.max(f, axis=2, keepdims=True))
            es, ef = jnp.exp(s - top), jnp.exp(f - top)
            total = jnp.sum(es, axis=2, keepdims=True) + jnp.sum(ef, axis=2, keepdims=True)
            inv = 1.0 / total
            ws_ = (es * inv).reshape(64, 512).astype(jnp.bfloat16)
            wf = (ef * inv).reshape(64, 16).astype(jnp.bfloat16)
            o = jnp.dot(ws_, vv[pl.ds(1024 * i + 512 * t, 512), :], preferred_element_type=jnp.float32)
            o = o + jnp.dot(wf, nv[top_rows, :], preferred_element_type=jnp.float32)
            halves.append(o)
        for h in range(GROUP):
            block = jnp.concatenate([o[8 * h : 8 * h + 8] for o in halves], axis=0)
            att[top_rows, pl.ds(128 * h, 128)] = block.astype(jnp.bfloat16)

    lane = lax.broadcasted_iota(jnp.int32, (8, 128), 1)
    lane_group = lane // RANK

    def place_rows():
        named = [spread(lambda r: ad[r], 8 * i) for i in range(8)]
        slot = jnp.concatenate([spread(lambda r: home[ad[r]], 8 * i) for i in range(8)], axis=0)
        named = jnp.concatenate(named, axis=0)
        row_lane = lax.broadcasted_iota(jnp.int32, (ROWS, 128), 1)
        hot = jnp.where(named == row_lane, 1.0, 0.0).astype(jnp.bfloat16)
        same = lax.dot_general(hot, hot, contract, preferred_element_type=jnp.float32)
        before = lax.broadcasted_iota(jnp.int32, (ROWS, ROWS), 1) < lax.broadcasted_iota(
            jnp.int32, (ROWS, ROWS), 0
        )
        twin = jnp.sum(jnp.where(before, same, 0.0), axis=1, keepdims=True) > 0.5
        c, xx, yy = (slot // 2) % 2, (slot // 4) % 4, slot // 16
        a, b = jnp.where(c == 0, xx, yy), jnp.where(c == 0, yy, xx)
        place = (((c * 4 + b) * 4 + a) * 2 + slot % 2) * 2 + twin.astype(jnp.int32)
        return jnp.where(place == row_lane, 1.0, 0.0).astype(jnp.bfloat16)

    def project(t):
        ws[t].wait()
        value = jnp.dot(att[...], w[t], preferred_element_type=jnp.float32)
        if t == 7:
            own[...] = value
            return
        rs_src[t] = value.astype(jnp.bfloat16)
        send(rs_src.at[t], rs_dst.at[z], rs_send.at[t], rs_recv.at[z], (req, other[t]))

    for i in (0, 3, 4, 5):
        loads[i].wait()
    attend(0)
    attend(1)
    pl.semaphore_wait(barrier, len(peers))

    loads[6].wait()
    loads[7].wait()
    pools = []
    for j, d in enumerate((1, 3, 2)):
        for p, pool in enumerate((pool_d, pool_u)):
            ref = pool.at[own_rows]
            pools.append(send(ref, ref, pool_send.at[p, j], pool_recv.at[p, j], peer_a(d)))
    loads[1].wait()
    loads[2].wait()
    place = place_rows()
    attend(2)
    attend(3)

    moved = lax.dot_general(place, att[...], (((0,), (0,)), ((), ())), preferred_element_type=jnp.float32)
    x_src[...] = moved.astype(jnp.bfloat16).reshape(8, 16, 1024)
    for kind in range(2):
        j = y if kind == 0 else x
        for d in (2, 1, 3):
            send(
                x_src.at[kind * 4 + (j + d) % 4], x_dst.at[core * 4 + j],
                x_send.at[kind * 3 + d - 1], x_recv.at[core * 3 + d - 1], owner(kind, d),
            )
    send(
        x_src.at[sib_bundle], x_dst.at[core * 4 + jnp.where(core == 0, x, y)], x_send.at[6], x_recv.at[6], sibling
    )
    x_dst[own_bundle] = x_src[own_bundle]

    project(0)
    project(1)
    project(2)
    project(3)

    for copy in pools:
        copy.wait_recv()
    for c in range(2):
        for d in range(1, 4):
            here = c * 4 + (b_me - d + 4) % 4
            received(x_src.at[0], x_dst.at[here], x_recv.at[c * 3 + d - 1])
    received(x_src.at[0], x_dst.at[sib_source], x_recv.at[6])

    inner = lax.dot_general(
        x_dst[...].reshape(128, 1024), pool_d[...], contract, preferred_element_type=jnp.float32
    )
    tall = lax.broadcasted_iota(jnp.int32, (128, 128), 0)
    wide_group = lax.broadcasted_iota(jnp.int32, (128, 128), 1) // RANK
    mine = wide_group == (tall % 16) // 2

    def fold(value):
        for shift in (64, 32, 16):
            value = value + pltpu.roll(value, shift, 1)
        return value

    inner = fold(jnp.where(mine, inner, 0.0))
    for half in range(2):
        packed = jnp.zeros((8, 128), jnp.float32)
        for i in range(8):
            row = 64 * half + 8 * i
            packed = jnp.where(lane_group == i, inner[row : row + 8], packed)
        low_own[pl.ds(8 * half, 8), :] = packed
    low_all[z] = low_own[...]
    for d in (4, 3, 5, 2, 6, 1, 7):
        send(low_own, low_all.at[z], low_send.at[d - 1], low_recv.at[d - 1], (req, (z + d) % 8))

    project(4)
    project(5)
    project(6)
    project(7)

    for d in range(1, 8):
        received(low_own, low_all.at[(z - d + 8) % 8], low_recv.at[d - 1])
    total = low_all[0]
    for j in range(1, 8):
        total = total + low_all[j]
    rows = [jnp.where(lane_group == i % 8, total[i // 8 * 8 : i // 8 * 8 + 8], 0.0) for i in range(16)]
    low = jnp.where(mine, fold(jnp.concatenate(rows, axis=0)), 0.0).astype(jnp.bfloat16)
    delta = jnp.dot(low, pool_u[...], preferred_element_type=jnp.float32)
    y_src[...] = delta.astype(jnp.bfloat16).reshape(8, 16, 512)

    for c in range(2):
        for d in (2, 1, 3):
            send(
                y_src.at[c * 4 + (b_me + d) % 4], y_dst.at[own_bundle],
                y_send.at[c * 3 + d - 1], y_recv.at[core * 3 + d - 1], source(c, d),
            )
    send(y_src.at[sib_source], y_dst.at[own_bundle], y_send.at[6], y_recv.at[6], sibling)
    y_dst[own_bundle] = y_src[own_bundle]

    value = own[...]
    for t in range(7):
        received(rs_src.at[t], rs_dst.at[other[t]], rs_recv.at[other[t]])
        value = value + rs_dst[other[t]].astype(jnp.float32)
    own[...] = value

    for kind in range(2):
        j = y if kind == 0 else x
        for d in range(1, 4):
            received(y_src.at[0], y_dst.at[kind * 4 + (j - d + 4) % 4], y_recv.at[kind * 3 + d - 1])
    received(y_src.at[0], y_dst.at[sib_bundle], y_recv.at[6])
    change = jnp.dot(place, y_dst[...].reshape(128, 512), preferred_element_type=jnp.float32)
    out_ref[...] = (own[...] + change).astype(jnp.bfloat16)
    for copy in started:
        copy.wait_send()


def per_device(
    queries, key_cache, value_cache, new_key, new_value, cache_length, row_adapter, adapter_home,
    down_pool, up_pool, out_weight,
):
    down = jnp.transpose(down_pool, (0, 2, 1)).reshape(32, 1024)
    up = up_pool.reshape(32, 512)
    keys = key_cache.reshape(4096, 128)
    values = value_cache.reshape(4096, 128)
    named = row_adapter.reshape(64)
    hbm = pl.BlockSpec(memory_space=pltpu.HBM)
    bf16 = jnp.bfloat16
    dma, vmem, smem = pltpu.SemaphoreType.DMA, pltpu.VMEM, pltpu.SMEM
    return pl.pallas_call(
        kernel,
        out_shape=jax.ShapeDtypeStruct((64, 512), bf16),
        in_specs=[hbm] * 11,
        out_specs=pl.BlockSpec(memory_space=pltpu.VMEM),
        scratch_shapes=[
            vmem((64, 1024), bf16),
            vmem((4096, 128), bf16),
            vmem((4096, 128), bf16),
            vmem((64, 128), bf16),
            vmem((64, 128), bf16),
            smem((64,), jnp.int32),
            smem((64,), jnp.int32),
            smem((64,), jnp.int32),
            vmem((128, 1024), bf16),
            vmem((128, 512), bf16),
            vmem((8, 1024, 512), bf16),
            vmem((64, 1024), bf16),
            vmem((64, 512), jnp.float32),
            vmem((7, 64, 512), bf16),
            vmem((8, 64, 512), bf16),
            vmem((8, 16, 1024), bf16),
            vmem((8, 16, 1024), bf16),
            vmem((16, 128), jnp.float32),
            vmem((8, 16, 128), jnp.float32),
            vmem((8, 16, 512), bf16),
            vmem((8, 16, 512), bf16),
            dma((8,)),
            dma((2, 4)),
            dma((8,)),
            dma((2, 3)),
            dma((2, 3)),
            dma((7,)),
            dma((7,)),
            dma((7,)),
            dma((7,)),
            dma((7,)),
            dma((7,)),
            dma((7,)),
            dma((8,)),
        ],
        compiler_params=pltpu.CompilerParams(
            collective_id=0, has_side_effects=True, vmem_limit_bytes=60 * 1024 * 1024
        ),
    )(
        queries, keys, values, new_key, new_value, cache_length, named, adapter_home, down, up, out_weight
    )


def solution(mesh):
    return jax.shard_map(
        per_device,
        mesh=mesh,
        in_specs=(
            P("req", "tp"),
            P("req", "tp", None, None),
            P("req", "tp", None, None),
            P("req", "tp"),
            P("req", "tp"),
            P("req"),
            P("req", None),
            P(),
            P("req", "tp", None),
            P("req", None, "tp"),
            P("tp", None),
        ),
        out_specs=P("req", "tp"),
        check_vma=False,
    )
```

```python
import jax
import jax.numpy as jnp
from jax import lax
from jax.experimental import pallas as pl
from jax.experimental.pallas import tpu as pltpu
from jax.sharding import PartitionSpec as P

MESH = pl.DeviceIdType.MESH
HEAD_DIM = 128
GROUP = 8
ROWS = 64
CACHE = 64
RANK = 16
NEG = -1e30
ORDER = (4, 3, 5, 1, 7, 2, 6, 0)


def kernel(
    q_hbm, k_hbm, v_hbm, nk_hbm, nv_hbm, len_hbm, ad_hbm, home_hbm, down_hbm, up_hbm, w_hbm,
    out_ref,
    q, kk, vv, nk, nv, lens, ad, home, pool_d, pool_u, w, att, part, rs_src, rs_dst,
    x_src, x_dst, low_own, low_all, y_src, y_dst,
    in_sem, kv_sem, w_sem, pool_send, pool_recv, x_send, x_recv, y_send, y_recv, low_send, low_recv,
    rs_send, rs_recv,
):
    req, z = lax.axis_index("req"), lax.axis_index("tp")
    core = req % 2
    x = (req // 2) % 4
    y = req // 8

    a_me = jnp.where(core == 0, x, y)
    b_me = jnp.where(core == 0, y, x)

    def at(yy, xx, cc):
        return ((yy % 4 * 4 + xx % 4) * 2 + cc, z)

    def peer_a(d):
        return at(y + core * d, x + (1 - core) * d, core)

    def owner(kind, d):
        return at(y + d, x, 0) if kind == 0 else at(y, x + d, 1)

    def source(kind, d):
        return at(y + (1 - core) * d, x + core * d, kind)

    sibling = at(y, x, 1 - core)
    own_bundle = core * 4 + b_me
    sib_bundle = jnp.where(core == 0, 4 + x, y)
    sib_source = (1 - core) * 4 + b_me

    own_rows = pl.ds(pl.multiple_of(a_me * 32, 32), 32)
    loads = [
        (len_hbm, lens), (ad_hbm, ad), (home_hbm, home), (q_hbm, q), (nk_hbm, nk), (nv_hbm, nv),
        (down_hbm, pool_d.at[own_rows]), (up_hbm, pool_u.at[own_rows]),
    ]
    loads = [pltpu.make_async_copy(s, d, in_sem.at[i]) for i, (s, d) in enumerate(loads)]
    for i in (0, 3, 4):
        loads[i].start()
    kv = []
    for i in range(4):
        rows = pl.ds(1024 * i, 1024)
        kv.append(pltpu.make_async_copy(k_hbm.at[rows], kk.at[rows], kv_sem.at[0, i]))
        kv.append(pltpu.make_async_copy(v_hbm.at[rows], vv.at[rows], kv_sem.at[1, i]))
    for c in kv[:2]:
        c.start()
    for i in (5, 6, 7, 1, 2):
        loads[i].start()
    for c in kv[2:]:
        c.start()
    ws = []
    for t, o in enumerate(ORDER):
        col = pl.multiple_of((z + o) % 8 * 512, 512)
        ws.append(pltpu.make_async_copy(w_hbm.at[:, pl.ds(col, 512)], w.at[t], w_sem.at[t]))
        ws[-1].start()

    barrier = pltpu.get_barrier_semaphore()
    peers = [sibling]
    for d in range(1, 4):
        for c in range(2):
            peers += [at(y + d, x, c), at(y, x + d, c)]
    peers += [(req, (z + d) % 8) for d in range(1, 8)]
    for p in peers:
        pl.semaphore_signal(barrier, inc=1, device_id=p, device_id_type=MESH)

    started = []

    def send(src, dst, send_sem, recv_sem, device):
        copy = pltpu.make_async_remote_copy(
            src_ref=src, dst_ref=dst, send_sem=send_sem, recv_sem=recv_sem, device_id=device, device_id_type=MESH
        )
        copy.start()
        started.append(copy)
        return copy

    def received(src, dst, recv_sem):
        pltpu.make_async_remote_copy(
            src_ref=src, dst_ref=dst, send_sem=low_send.at[0], recv_sem=recv_sem, device_id=sibling,
            device_id_type=MESH,
        ).wait_recv()

    scale = 1.0 / HEAD_DIM**0.5
    sub = lax.broadcasted_iota(jnp.int32, (8, 128), 0)
    sub_wide = lax.broadcasted_iota(jnp.int32, (8, 512), 0)
    lane_wide = lax.broadcasted_iota(jnp.int32, (8, 512), 1)
    sub_new = lax.broadcasted_iota(jnp.int32, (8, 16), 0)
    lane_new = lax.broadcasted_iota(jnp.int32, (8, 16), 1)
    contract = (((1,), (1,)), ((), ()))

    def spread(read, base):
        values = jnp.zeros((8, 128), jnp.int32)
        for r in range(8):
            values = jnp.where(sub == r, read(base + r), values)
        return values

    def attend(i):
        top_rows = pl.ds(16 * i, 16)
        queries = jnp.concatenate([q[top_rows, pl.ds(128 * h, 128)] for h in range(GROUP)], axis=0)
        keys = kk[pl.ds(1024 * i, 1024), :]
        scores = lax.dot_general(queries, keys, contract, preferred_element_type=jnp.float32)
        fresh = lax.dot_general(queries, nk[top_rows, :], contract, preferred_element_type=jnp.float32)
        scores = scores.reshape(8, 2, 8, 1024)
        fresh = fresh.reshape(8, 2, 8, 16)
        halves = []
        for t in range(2):
            base = 16 * i + 8 * t
            count = spread(lambda r: lens[r], base)[:, :1]
            valid = (lane_wide // CACHE == sub_wide) & (lane_wide % CACHE < count)
            mine = lane_new == sub_new + 8 * t
            s = jnp.where(valid[None], scores[:, t, :, 512 * t : 512 * t + 512] * scale, NEG)
            f = jnp.where(mine[None], fresh[:, t] * scale, NEG)
            top = jnp.maximum(jnp.max(s, axis=2, keepdims=True), jnp.max(f, axis=2, keepdims=True))
            es, ef = jnp.exp(s - top), jnp.exp(f - top)
            total = jnp.sum(es, axis=2, keepdims=True) + jnp.sum(ef, axis=2, keepdims=True)
            inv = 1.0 / total
            ws_ = (es * inv).reshape(64, 512).astype(jnp.bfloat16)
            wf = (ef * inv).reshape(64, 16).astype(jnp.bfloat16)
            o = jnp.dot(ws_, vv[pl.ds(1024 * i + 512 * t, 512), :], preferred_element_type=jnp.float32)
            o = o + jnp.dot(wf, nv[top_rows, :], preferred_element_type=jnp.float32)
            halves.append(o)
        for h in range(GROUP):
            block = jnp.concatenate([o[8 * h : 8 * h + 8] for o in halves], axis=0)
            att[top_rows, pl.ds(128 * h, 128)] = block.astype(jnp.bfloat16)

    lane = lax.broadcasted_iota(jnp.int32, (8, 128), 1)
    lane_group = lane // RANK

    def place_rows():
        named = [spread(lambda r: ad[r], 8 * i) for i in range(8)]
        slot = jnp.concatenate([spread(lambda r: home[ad[r]], 8 * i) for i in range(8)], axis=0)
        named = jnp.concatenate(named, axis=0)
        row_lane = lax.broadcasted_iota(jnp.int32, (ROWS, 128), 1)
        hot = jnp.where(named == row_lane, 1.0, 0.0).astype(jnp.bfloat16)
        same = lax.dot_general(hot, hot, contract, preferred_element_type=jnp.float32)
        before = lax.broadcasted_iota(jnp.int32, (ROWS, ROWS), 1) < lax.broadcasted_iota(
            jnp.int32, (ROWS, ROWS), 0
        )
        twin = jnp.sum(jnp.where(before, same, 0.0), axis=1, keepdims=True) > 0.5
        c, xx, yy = (slot // 2) % 2, (slot // 4) % 4, slot // 16
        a, b = jnp.where(c == 0, xx, yy), jnp.where(c == 0, yy, xx)
        place = (((c * 4 + b) * 4 + a) * 2 + slot % 2) * 2 + twin.astype(jnp.int32)
        return jnp.where(place == row_lane, 1.0, 0.0).astype(jnp.bfloat16)

    def project(first, last):
        for t in range(first, last):
            ws[t].wait()

        def step(t, carry):
            part[t] = jnp.dot(att[...], w[t], preferred_element_type=jnp.float32)
            return carry

        lax.fori_loop(first, last, step, 0)

    def along(d):
        return (req, (z + d) % 8)

    def sum_copy(j, way, d):
        return send(rs_src.at[j, way], rs_dst.at[j, way], rs_send.at[j, way], rs_recv.at[j, way], along(d))

    def first_sums():
        far = []
        for way, d in enumerate((2, 6)):
            cols = pl.ds(256 * way, 256)
            rs_src[0, way, :, cols] = part[0, :, cols].astype(jnp.bfloat16)
            far.append(
                send(
                    rs_src.at[0, way, :, cols], rs_dst.at[0, way, :, cols], rs_send.at[0, way], rs_recv.at[0, way],
                    along(d),
                )
            )
        for way, d in enumerate((1, 7)):
            rs_src[1, way] = part[1 + way].astype(jnp.bfloat16)
            far.append(sum_copy(1, way, d))
        near = []
        for way, d in enumerate((1, 7)):
            rs_src[2, way] = part[3 + way].astype(jnp.bfloat16)
            near.append(sum_copy(2, way, d))
        return far, near

    def second_sums(far):
        for copy in far:
            copy.wait_recv()
        last = []
        for way, d in enumerate((2, 6)):
            for half in range(2):
                cols = pl.ds(256 * half, 256)
                value = part[5 + way, :, cols] + rs_dst[1, way, :, cols].astype(jnp.float32)
                if half == way:
                    value = value + rs_dst[0, way, :, cols].astype(jnp.float32)
                rs_src[3, way, :, cols] = value.astype(jnp.bfloat16)
            last.append(sum_copy(3, way, d))
        return last

    for i in (1, 2):
        loads[i].wait()
    place = place_rows()
    pl.semaphore_wait(barrier, len(peers))

    loads[6].wait()
    loads[7].wait()
    pools = []
    for p, pool in enumerate((pool_d, pool_u)):
        for j, d in enumerate((2, 1, 3)):
            ref = pool.at[own_rows]
            pools.append(send(ref, ref, pool_send.at[p, j], pool_recv.at[p, j], peer_a(d)))

    for i in (0, 3, 4, 5):
        loads[i].wait()
    for c in kv:
        c.wait()
    for i in range(4):
        attend(i)

    moved = lax.dot_general(place, att[...], (((0,), (0,)), ((), ())), preferred_element_type=jnp.float32)
    x_src[...] = moved.astype(jnp.bfloat16).reshape(8, 16, 1024)
    for kind in range(2):
        j = y if kind == 0 else x
        for d in (2, 1, 3):
            send(
                x_src.at[kind * 4 + (j + d) % 4], x_dst.at[core * 4 + j],
                x_send.at[kind * 3 + d - 1], x_recv.at[core * 3 + d - 1], owner(kind, d),
            )
    send(
        x_src.at[sib_bundle], x_dst.at[core * 4 + jnp.where(core == 0, x, y)], x_send.at[6], x_recv.at[6], sibling
    )
    x_dst[own_bundle] = x_src[own_bundle]

    project(0, 5)
    far, near = first_sums()

    for copy in pools[:3]:
        copy.wait_recv()
    for c in range(2):
        for d in range(1, 4):
            here = c * 4 + (b_me - d + 4) % 4
            received(x_src.at[0], x_dst.at[here], x_recv.at[c * 3 + d - 1])
    received(x_src.at[0], x_dst.at[sib_source], x_recv.at[6])

    inner = lax.dot_general(
        x_dst[...].reshape(128, 1024), pool_d[...], contract, preferred_element_type=jnp.float32
    )
    tall = lax.broadcasted_iota(jnp.int32, (128, 128), 0)
    wide_group = lax.broadcasted_iota(jnp.int32, (128, 128), 1) // RANK
    mine = wide_group == (tall % 16) // 2

    def fold(value):
        for shift in (64, 32, 16):
            value = value + pltpu.roll(value, shift, 1)
        return value

    inner = fold(jnp.where(mine, inner, 0.0))
    for half in range(2):
        packed = jnp.zeros((8, 128), jnp.float32)
        for i in range(8):
            row = 64 * half + 8 * i
            packed = jnp.where(lane_group == i, inner[row : row + 8], packed)
        low_own[pl.ds(8 * half, 8), :] = packed
    low_all[z] = low_own[...]
    for d in (4, 3, 5, 2, 6, 1, 7):
        send(low_own, low_all.at[z], low_send.at[d - 1], low_recv.at[d - 1], (req, (z + d) % 8))

    project(5, 8)
    last = second_sums(far)

    for d in range(1, 8):
        received(low_own, low_all.at[(z - d + 8) % 8], low_recv.at[d - 1])
    total = low_all[0]
    for j in range(1, 8):
        total = total + low_all[j]
    rows = [jnp.where(lane_group == i % 8, total[i // 8 * 8 : i // 8 * 8 + 8], 0.0) for i in range(16)]
    for copy in pools[3:]:
        copy.wait_recv()
    low = jnp.where(mine, fold(jnp.concatenate(rows, axis=0)), 0.0).astype(jnp.bfloat16)
    delta = jnp.dot(low, pool_u[...], preferred_element_type=jnp.float32)
    y_src[...] = delta.astype(jnp.bfloat16).reshape(8, 16, 512)

    for c in range(2):
        for d in (2, 1, 3):
            send(
                y_src.at[c * 4 + (b_me + d) % 4], y_dst.at[own_bundle],
                y_send.at[c * 3 + d - 1], y_recv.at[core * 3 + d - 1], source(c, d),
            )
    send(y_src.at[sib_source], y_dst.at[own_bundle], y_send.at[6], y_recv.at[6], sibling)
    y_dst[own_bundle] = y_src[own_bundle]

    for j, copies in ((2, near), (3, last)):
        for way, copy in enumerate(copies):
            copy.wait_recv()
            part[7] = part[7] + rs_dst[j, way].astype(jnp.float32)

    for kind in range(2):
        j = y if kind == 0 else x
        for d in range(1, 4):
            received(y_src.at[0], y_dst.at[kind * 4 + (j - d + 4) % 4], y_recv.at[kind * 3 + d - 1])
    received(y_src.at[0], y_dst.at[sib_bundle], y_recv.at[6])
    change = jnp.dot(place, y_dst[...].reshape(128, 512), preferred_element_type=jnp.float32)
    out_ref[...] = (part[7] + change).astype(jnp.bfloat16)
    for copy in started:
        copy.wait_send()


def per_device(
    queries, key_cache, value_cache, new_key, new_value, cache_length, row_adapter, adapter_home,
    down_pool, up_pool, out_weight,
):
    down = jnp.transpose(down_pool, (0, 2, 1)).reshape(32, 1024)
    up = up_pool.reshape(32, 512)
    keys = key_cache.reshape(4096, 128)
    values = value_cache.reshape(4096, 128)
    named = row_adapter.reshape(64)
    hbm = pl.BlockSpec(memory_space=pltpu.HBM)
    bf16 = jnp.bfloat16
    dma, vmem, smem = pltpu.SemaphoreType.DMA, pltpu.VMEM, pltpu.SMEM
    return pl.pallas_call(
        kernel,
        out_shape=jax.ShapeDtypeStruct((64, 512), bf16),
        in_specs=[hbm] * 11,
        out_specs=pl.BlockSpec(memory_space=pltpu.VMEM),
        scratch_shapes=[
            vmem((64, 1024), bf16),
            vmem((4096, 128), bf16),
            vmem((4096, 128), bf16),
            vmem((64, 128), bf16),
            vmem((64, 128), bf16),
            smem((64,), jnp.int32),
            smem((64,), jnp.int32),
            smem((64,), jnp.int32),
            vmem((128, 1024), bf16),
            vmem((128, 512), bf16),
            vmem((8, 1024, 512), bf16),
            vmem((64, 1024), bf16),
            vmem((8, 64, 512), jnp.float32),
            vmem((4, 2, 64, 512), bf16),
            vmem((4, 2, 64, 512), bf16),
            vmem((8, 16, 1024), bf16),
            vmem((8, 16, 1024), bf16),
            vmem((16, 128), jnp.float32),
            vmem((8, 16, 128), jnp.float32),
            vmem((8, 16, 512), bf16),
            vmem((8, 16, 512), bf16),
            dma((8,)),
            dma((2, 4)),
            dma((8,)),
            dma((2, 3)),
            dma((2, 3)),
            dma((7,)),
            dma((7,)),
            dma((7,)),
            dma((7,)),
            dma((7,)),
            dma((7,)),
            dma((4, 2)),
            dma((4, 2)),
        ],
        compiler_params=pltpu.CompilerParams(
            collective_id=0, has_side_effects=True, vmem_limit_bytes=60 * 1024 * 1024
        ),
    )(
        queries, keys, values, new_key, new_value, cache_length, named, adapter_home, down, up, out_weight
    )


def solution(mesh):
    return jax.shard_map(
        per_device,
        mesh=mesh,
        in_specs=(
            P("req", "tp"),
            P("req", "tp", None, None),
            P("req", "tp", None, None),
            P("req", "tp"),
            P("req", "tp"),
            P("req"),
            P("req", None),
            P(),
            P("req", "tp", None),
            P("req", None, "tp"),
            P("tp", None),
        ),
        out_specs=P("req", "tp"),
        check_vma=False,
    )
```

```python
import jax
import jax.numpy as jnp
from jax import lax
from jax.experimental import pallas as pl
from jax.experimental.pallas import tpu as pltpu
from jax.sharding import PartitionSpec as P

MESH = pl.DeviceIdType.MESH
HEAD_DIM = 128
GROUP = 8
ROWS = 64
CACHE = 64
RANK = 16
NEG = -1e30
ORDER = (4, 3, 5, 1, 7, 2, 6, 0)


def kernel(
    q_hbm, k_hbm, v_hbm, nk_hbm, nv_hbm, len_hbm, ad_hbm, home_hbm, down_hbm, up_hbm, w_hbm,
    out_ref,
    q, kk, vv, nk, nv, lens, ad, home, pool_d, pool_u, w, att, part, rs_src, rs_dst,
    x_src, x_dst, low_own, low_all, y_src, y_dst,
    in_sem, kv_sem, w_sem, pool_send, pool_recv, x_send, x_recv, y_send, y_recv, low_send, low_recv,
    rs_send, rs_recv,
):
    req, z = lax.axis_index("req"), lax.axis_index("tp")
    core = req % 2
    x = (req // 2) % 4
    y = req // 8

    a_me = jnp.where(core == 0, x, y)
    b_me = jnp.where(core == 0, y, x)

    def at(yy, xx, cc):
        return ((yy % 4 * 4 + xx % 4) * 2 + cc, z)

    def peer_a(d):
        return at(y + core * d, x + (1 - core) * d, core)

    def owner(kind, d):
        return at(y + d, x, 0) if kind == 0 else at(y, x + d, 1)

    def source(kind, d):
        return at(y + (1 - core) * d, x + core * d, kind)

    sibling = at(y, x, 1 - core)
    own_bundle = core * 4 + b_me
    sib_bundle = jnp.where(core == 0, 4 + x, y)
    sib_source = (1 - core) * 4 + b_me

    own_rows = pl.ds(pl.multiple_of(a_me * 32, 32), 32)
    loads = [
        (len_hbm, lens), (ad_hbm, ad), (home_hbm, home), (q_hbm, q), (nk_hbm, nk), (nv_hbm, nv),
        (down_hbm, pool_d.at[own_rows]), (up_hbm, pool_u.at[own_rows]),
    ]
    loads = [pltpu.make_async_copy(s, d, in_sem.at[i]) for i, (s, d) in enumerate(loads)]
    for i in (0, 3, 4):
        loads[i].start()
    kv = []
    for i in range(4):
        rows = pl.ds(1024 * i, 1024)
        kv.append(pltpu.make_async_copy(k_hbm.at[rows], kk.at[rows], kv_sem.at[0, i]))
        kv.append(pltpu.make_async_copy(v_hbm.at[rows], vv.at[rows], kv_sem.at[1, i]))
    for c in kv[:2]:
        c.start()
    for i in (5, 6, 7, 1, 2):
        loads[i].start()
    for c in kv[2:]:
        c.start()
    ws = []
    for t, o in enumerate(ORDER):
        col = pl.multiple_of((z + o) % 8 * 512, 512)
        ws.append(pltpu.make_async_copy(w_hbm.at[:, pl.ds(col, 512)], w.at[t], w_sem.at[t]))

    barrier = pltpu.get_barrier_semaphore()
    peers = [sibling]
    for d in range(1, 4):
        for c in range(2):
            peers += [at(y + d, x, c), at(y, x + d, c)]
    peers += [(req, (z + d) % 8) for d in range(1, 8)]
    for p in peers:
        pl.semaphore_signal(barrier, inc=1, device_id=p, device_id_type=MESH)

    started = []

    def send(src, dst, send_sem, recv_sem, device):
        copy = pltpu.make_async_remote_copy(
            src_ref=src, dst_ref=dst, send_sem=send_sem, recv_sem=recv_sem, device_id=device, device_id_type=MESH
        )
        copy.start()
        started.append(copy)
        return copy

    def received(src, dst, recv_sem):
        pltpu.make_async_remote_copy(
            src_ref=src, dst_ref=dst, send_sem=low_send.at[0], recv_sem=recv_sem, device_id=sibling,
            device_id_type=MESH,
        ).wait_recv()

    scale = 1.0 / HEAD_DIM**0.5
    sub = lax.broadcasted_iota(jnp.int32, (8, 128), 0)
    sub_wide = lax.broadcasted_iota(jnp.int32, (8, 512), 0)
    lane_wide = lax.broadcasted_iota(jnp.int32, (8, 512), 1)
    sub_new = lax.broadcasted_iota(jnp.int32, (8, 16), 0)
    lane_new = lax.broadcasted_iota(jnp.int32, (8, 16), 1)
    contract = (((1,), (1,)), ((), ()))

    def spread(read, base):
        values = jnp.zeros((8, 128), jnp.int32)
        for r in range(8):
            values = jnp.where(sub == r, read(base + r), values)
        return values

    def attend(i):
        top_rows = pl.ds(16 * i, 16)
        queries = jnp.concatenate([q[top_rows, pl.ds(128 * h, 128)] for h in range(GROUP)], axis=0)
        keys = kk[pl.ds(1024 * i, 1024), :]
        scores = lax.dot_general(queries, keys, contract, preferred_element_type=jnp.float32)
        fresh = lax.dot_general(queries, nk[top_rows, :], contract, preferred_element_type=jnp.float32)
        scores = scores.reshape(8, 2, 8, 1024)
        fresh = fresh.reshape(8, 2, 8, 16)
        halves = []
        for t in range(2):
            base = 16 * i + 8 * t
            count = spread(lambda r: lens[r], base)[:, :1]
            valid = (lane_wide // CACHE == sub_wide) & (lane_wide % CACHE < count)
            mine = lane_new == sub_new + 8 * t
            s = jnp.where(valid[None], scores[:, t, :, 512 * t : 512 * t + 512] * scale, NEG)
            f = jnp.where(mine[None], fresh[:, t] * scale, NEG)
            top = jnp.maximum(jnp.max(s, axis=2, keepdims=True), jnp.max(f, axis=2, keepdims=True))
            es, ef = jnp.exp(s - top), jnp.exp(f - top)
            total = jnp.sum(es, axis=2, keepdims=True) + jnp.sum(ef, axis=2, keepdims=True)
            inv = 1.0 / total
            ws_ = (es * inv).reshape(64, 512).astype(jnp.bfloat16)
            wf = (ef * inv).reshape(64, 16).astype(jnp.bfloat16)
            o = jnp.dot(ws_, vv[pl.ds(1024 * i + 512 * t, 512), :], preferred_element_type=jnp.float32)
            o = o + jnp.dot(wf, nv[top_rows, :], preferred_element_type=jnp.float32)
            halves.append(o)
        for h in range(GROUP):
            block = jnp.concatenate([o[8 * h : 8 * h + 8] for o in halves], axis=0)
            att[top_rows, pl.ds(128 * h, 128)] = block.astype(jnp.bfloat16)

    lane = lax.broadcasted_iota(jnp.int32, (8, 128), 1)
    lane_group = lane // RANK

    def place_rows():
        named = [spread(lambda r: ad[r], 8 * i) for i in range(8)]
        slot = jnp.concatenate([spread(lambda r: home[ad[r]], 8 * i) for i in range(8)], axis=0)
        named = jnp.concatenate(named, axis=0)
        row_lane = lax.broadcasted_iota(jnp.int32, (ROWS, 128), 1)
        hot = jnp.where(named == row_lane, 1.0, 0.0).astype(jnp.bfloat16)
        same = lax.dot_general(hot, hot, contract, preferred_element_type=jnp.float32)
        before = lax.broadcasted_iota(jnp.int32, (ROWS, ROWS), 1) < lax.broadcasted_iota(
            jnp.int32, (ROWS, ROWS), 0
        )
        twin = jnp.sum(jnp.where(before, same, 0.0), axis=1, keepdims=True) > 0.5
        c, xx, yy = (slot // 2) % 2, (slot // 4) % 4, slot // 16
        a, b = jnp.where(c == 0, xx, yy), jnp.where(c == 0, yy, xx)
        place = (((c * 4 + b) * 4 + a) * 2 + slot % 2) * 2 + twin.astype(jnp.int32)
        return jnp.where(place == row_lane, 1.0, 0.0).astype(jnp.bfloat16)

    def project(first, last):
        for t in range(first, last):
            ws[t].wait()

        def step(t, carry):
            part[t] = jnp.dot(att[...], w[t], preferred_element_type=jnp.float32)
            return carry

        lax.fori_loop(first, last, step, 0)

    def along(d):
        return (req, (z + d) % 8)

    def sum_copy(j, way, d):
        return send(rs_src.at[j, way], rs_dst.at[j, way], rs_send.at[j, way], rs_recv.at[j, way], along(d))

    def first_sums():
        far = []
        for way, d in enumerate((2, 6)):
            cols = pl.ds(256 * way, 256)
            rs_src[0, way, :, cols] = part[0, :, cols].astype(jnp.bfloat16)
            far.append(
                send(
                    rs_src.at[0, way, :, cols], rs_dst.at[0, way, :, cols], rs_send.at[0, way], rs_recv.at[0, way],
                    along(d),
                )
            )
        for way, d in enumerate((1, 7)):
            rs_src[1, way] = part[1 + way].astype(jnp.bfloat16)
            far.append(sum_copy(1, way, d))
        return far

    def near_sums():
        near = []
        for way, d in enumerate((1, 7)):
            rs_src[2, way] = part[3 + way].astype(jnp.bfloat16)
            near.append(sum_copy(2, way, d))
        return near

    def second_sums(far):
        for copy in far:
            copy.wait_recv()
        last = []
        for way, d in enumerate((2, 6)):
            for half in range(2):
                cols = pl.ds(256 * half, 256)
                value = part[5 + way, :, cols] + rs_dst[1, way, :, cols].astype(jnp.float32)
                if half == way:
                    value = value + rs_dst[0, way, :, cols].astype(jnp.float32)
                rs_src[3, way, :, cols] = value.astype(jnp.bfloat16)
            last.append(sum_copy(3, way, d))
        return last

    for i in (0, 3, 4, 5):
        loads[i].wait()
    for c in kv[:4]:
        c.wait()
    attend(0)
    attend(1)
    pl.semaphore_wait(barrier, len(peers))

    loads[6].wait()
    loads[7].wait()
    pools = []
    for p, pool in enumerate((pool_d, pool_u)):
        for j, d in enumerate((2, 1, 3)):
            ref = pool.at[own_rows]
            pools.append(send(ref, ref, pool_send.at[p, j], pool_recv.at[p, j], peer_a(d)))
    for c in ws:
        c.start()

    for i in (1, 2):
        loads[i].wait()
    for c in kv[4:]:
        c.wait()
    place = place_rows()
    attend(2)
    attend(3)

    moved = lax.dot_general(place, att[...], (((0,), (0,)), ((), ())), preferred_element_type=jnp.float32)
    x_src[...] = moved.astype(jnp.bfloat16).reshape(8, 16, 1024)
    for kind in range(2):
        j = y if kind == 0 else x
        for d in (2, 1, 3):
            send(
                x_src.at[kind * 4 + (j + d) % 4], x_dst.at[core * 4 + j],
                x_send.at[kind * 3 + d - 1], x_recv.at[core * 3 + d - 1], owner(kind, d),
            )
    send(
        x_src.at[sib_bundle], x_dst.at[core * 4 + jnp.where(core == 0, x, y)], x_send.at[6], x_recv.at[6], sibling
    )
    x_dst[own_bundle] = x_src[own_bundle]

    project(0, 5)
    far = first_sums()

    for copy in pools[:3]:
        copy.wait_recv()
    for c in range(2):
        for d in range(1, 4):
            here = c * 4 + (b_me - d + 4) % 4
            received(x_src.at[0], x_dst.at[here], x_recv.at[c * 3 + d - 1])
    received(x_src.at[0], x_dst.at[sib_source], x_recv.at[6])

    inner = lax.dot_general(
        x_dst[...].reshape(128, 1024), pool_d[...], contract, preferred_element_type=jnp.float32
    )
    tall = lax.broadcasted_iota(jnp.int32, (128, 128), 0)
    wide_group = lax.broadcasted_iota(jnp.int32, (128, 128), 1) // RANK
    mine = wide_group == (tall % 16) // 2

    def fold(value):
        for shift in (64, 32, 16):
            value = value + pltpu.roll(value, shift, 1)
        return value

    inner = fold(jnp.where(mine, inner, 0.0))
    halves = []
    for half in range(2):
        packed = jnp.zeros((8, 128), jnp.float32)
        for i in range(8):
            row = 64 * half + 8 * i
            packed = jnp.where(lane_group == i, inner[row : row + 8], packed)
        halves.append(packed)
    low_own[...] = jnp.concatenate(halves, axis=0).astype(jnp.bfloat16)
    low_all[z] = low_own[...]
    for d in (4, 3, 5, 2, 6, 1, 7):
        send(low_own, low_all.at[z], low_send.at[d - 1], low_recv.at[d - 1], (req, (z + d) % 8))

    near = near_sums()
    project(5, 8)
    last = second_sums(far)

    for d in range(1, 8):
        received(low_own, low_all.at[(z - d + 8) % 8], low_recv.at[d - 1])
    total = low_all[0].astype(jnp.float32)
    for j in range(1, 8):
        total = total + low_all[j].astype(jnp.float32)
    rows = [jnp.where(lane_group == i % 8, total[i // 8 * 8 : i // 8 * 8 + 8], 0.0) for i in range(16)]
    for copy in pools[3:]:
        copy.wait_recv()
    low = jnp.where(mine, fold(jnp.concatenate(rows, axis=0)), 0.0).astype(jnp.bfloat16)
    delta = jnp.dot(low, pool_u[...], preferred_element_type=jnp.float32)
    y_src[...] = delta.astype(jnp.bfloat16).reshape(8, 16, 512)

    for c in range(2):
        for d in (2, 1, 3):
            send(
                y_src.at[c * 4 + (b_me + d) % 4], y_dst.at[own_bundle],
                y_send.at[c * 3 + d - 1], y_recv.at[core * 3 + d - 1], source(c, d),
            )
    send(y_src.at[sib_source], y_dst.at[own_bundle], y_send.at[6], y_recv.at[6], sibling)
    y_dst[own_bundle] = y_src[own_bundle]

    for j, copies in ((2, near), (3, last)):
        for way, copy in enumerate(copies):
            copy.wait_recv()
            part[7] = part[7] + rs_dst[j, way].astype(jnp.float32)

    for kind in range(2):
        j = y if kind == 0 else x
        for d in range(1, 4):
            received(y_src.at[0], y_dst.at[kind * 4 + (j - d + 4) % 4], y_recv.at[kind * 3 + d - 1])
    received(y_src.at[0], y_dst.at[sib_bundle], y_recv.at[6])
    change = jnp.dot(place, y_dst[...].reshape(128, 512), preferred_element_type=jnp.float32)
    out_ref[...] = (part[7] + change).astype(jnp.bfloat16)
    for copy in started:
        copy.wait_send()


def per_device(
    queries, key_cache, value_cache, new_key, new_value, cache_length, row_adapter, adapter_home,
    down_pool, up_pool, out_weight,
):
    down = jnp.transpose(down_pool, (0, 2, 1)).reshape(32, 1024)
    up = up_pool.reshape(32, 512)
    keys = key_cache.reshape(4096, 128)
    values = value_cache.reshape(4096, 128)
    named = row_adapter.reshape(64)
    hbm = pl.BlockSpec(memory_space=pltpu.HBM)
    bf16 = jnp.bfloat16
    dma, vmem, smem = pltpu.SemaphoreType.DMA, pltpu.VMEM, pltpu.SMEM
    return pl.pallas_call(
        kernel,
        out_shape=jax.ShapeDtypeStruct((64, 512), bf16),
        in_specs=[hbm] * 11,
        out_specs=pl.BlockSpec(memory_space=pltpu.VMEM),
        scratch_shapes=[
            vmem((64, 1024), bf16),
            vmem((4096, 128), bf16),
            vmem((4096, 128), bf16),
            vmem((64, 128), bf16),
            vmem((64, 128), bf16),
            smem((64,), jnp.int32),
            smem((64,), jnp.int32),
            smem((64,), jnp.int32),
            vmem((128, 1024), bf16),
            vmem((128, 512), bf16),
            vmem((8, 1024, 512), bf16),
            vmem((64, 1024), bf16),
            vmem((8, 64, 512), jnp.float32),
            vmem((4, 2, 64, 512), bf16),
            vmem((4, 2, 64, 512), bf16),
            vmem((8, 16, 1024), bf16),
            vmem((8, 16, 1024), bf16),
            vmem((16, 128), bf16),
            vmem((8, 16, 128), bf16),
            vmem((8, 16, 512), bf16),
            vmem((8, 16, 512), bf16),
            dma((8,)),
            dma((2, 4)),
            dma((8,)),
            dma((2, 3)),
            dma((2, 3)),
            dma((7,)),
            dma((7,)),
            dma((7,)),
            dma((7,)),
            dma((7,)),
            dma((7,)),
            dma((4, 2)),
            dma((4, 2)),
        ],
        compiler_params=pltpu.CompilerParams(
            collective_id=0, has_side_effects=True, vmem_limit_bytes=60 * 1024 * 1024
        ),
    )(
        queries, keys, values, new_key, new_value, cache_length, named, adapter_home, down, up, out_weight
    )


def solution(mesh):
    return jax.shard_map(
        per_device,
        mesh=mesh,
        in_specs=(
            P("req", "tp"),
            P("req", "tp", None, None),
            P("req", "tp", None, None),
            P("req", "tp"),
            P("req", "tp"),
            P("req"),
            P("req", None),
            P(),
            P("req", "tp", None),
            P("req", None, "tp"),
            P("tp", None),
        ),
        out_specs=P("req", "tp"),
        check_vma=False,
    )
```

```python
import jax
import jax.numpy as jnp
from jax import lax
from jax.experimental import pallas as pl
from jax.experimental.pallas import tpu as pltpu
from jax.sharding import PartitionSpec as P

MESH = pl.DeviceIdType.MESH
HEAD_DIM = 128
GROUP = 8
ROWS = 64
CACHE = 64
RANK = 16
NEG = -1e30
ORDER = (4, 3, 5, 1, 7, 2, 6, 0)


def kernel(
    q_hbm, k_hbm, v_hbm, nk_hbm, nv_hbm, len_hbm, ad_hbm, home_hbm, down_hbm, up_hbm, w_hbm,
    out_ref,
    q, kk, vv, nk, nv, lens, ad, home, pool_d, pool_u, w, att, part, rs_src, rs_dst,
    x_src, x_dst, low_own, low_all, y_src, y_dst,
    in_sem, kv_sem, w_sem, pool_send, pool_recv, x_send, x_recv, y_send, y_recv, low_send, low_recv,
    rs_send, rs_recv,
):
    req, z = lax.axis_index("req"), lax.axis_index("tp")
    core = req % 2
    x = (req // 2) % 4
    y = req // 8

    a_me = jnp.where(core == 0, x, y)
    b_me = jnp.where(core == 0, y, x)

    def at(yy, xx, cc):
        return ((yy % 4 * 4 + xx % 4) * 2 + cc, z)

    def peer_a(d):
        return at(y + core * d, x + (1 - core) * d, core)

    def owner(kind, d):
        return at(y + d, x, 0) if kind == 0 else at(y, x + d, 1)

    def source(kind, d):
        return at(y + (1 - core) * d, x + core * d, kind)

    sibling = at(y, x, 1 - core)
    own_bundle = core * 4 + b_me
    sib_bundle = jnp.where(core == 0, 4 + x, y)
    sib_source = (1 - core) * 4 + b_me

    barrier = pltpu.get_barrier_semaphore()
    peers = [(req, (z + d) % 8) for d in (4, 3, 5, 2, 6, 1, 7)] + [sibling]
    for d in (2, 1, 3):
        for c in range(2):
            peers += [at(y + d, x, c), at(y, x + d, c)]
    for p in peers:
        pl.semaphore_signal(barrier, inc=1, device_id=p, device_id_type=MESH)

    own_rows = pl.ds(pl.multiple_of(a_me * 32, 32), 32)
    loads = [
        (len_hbm, lens), (ad_hbm, ad), (home_hbm, home), (q_hbm, q), (nk_hbm, nk), (nv_hbm, nv),
        (down_hbm, pool_d.at[own_rows]), (up_hbm, pool_u.at[own_rows]),
    ]
    loads = [pltpu.make_async_copy(s, d, in_sem.at[i]) for i, (s, d) in enumerate(loads)]
    for i in (0, 3, 4):
        loads[i].start()
    kv = []
    for i in range(4):
        rows = pl.ds(1024 * i, 1024)
        kv.append(pltpu.make_async_copy(k_hbm.at[rows], kk.at[rows], kv_sem.at[0, i]))
        kv.append(pltpu.make_async_copy(v_hbm.at[rows], vv.at[rows], kv_sem.at[1, i]))
    for c in kv[:2]:
        c.start()
    for i in (5, 6, 7, 1, 2):
        loads[i].start()
    for c in kv[2:]:
        c.start()
    ws = []
    for t, o in enumerate(ORDER):
        col = pl.multiple_of((z + o) % 8 * 512, 512)
        ws.append(pltpu.make_async_copy(w_hbm.at[:, pl.ds(col, 512)], w.at[t], w_sem.at[t]))

    started = []

    def send(src, dst, send_sem, recv_sem, device):
        copy = pltpu.make_async_remote_copy(
            src_ref=src, dst_ref=dst, send_sem=send_sem, recv_sem=recv_sem, device_id=device, device_id_type=MESH
        )
        copy.start()
        started.append(copy)
        return copy

    def received(src, dst, recv_sem):
        pltpu.make_async_remote_copy(
            src_ref=src, dst_ref=dst, send_sem=low_send.at[0], recv_sem=recv_sem, device_id=sibling,
            device_id_type=MESH,
        ).wait_recv()

    scale = 1.0 / HEAD_DIM**0.5
    sub = lax.broadcasted_iota(jnp.int32, (8, 128), 0)
    sub_wide = lax.broadcasted_iota(jnp.int32, (8, 512), 0)
    lane_wide = lax.broadcasted_iota(jnp.int32, (8, 512), 1)
    sub_new = lax.broadcasted_iota(jnp.int32, (8, 16), 0)
    lane_new = lax.broadcasted_iota(jnp.int32, (8, 16), 1)
    contract = (((1,), (1,)), ((), ()))

    def spread(read, base):
        values = jnp.zeros((8, 128), jnp.int32)
        for r in range(8):
            values = jnp.where(sub == r, read(base + r), values)
        return values

    def attend(i):
        top_rows = pl.ds(16 * i, 16)
        queries = jnp.concatenate([q[top_rows, pl.ds(128 * h, 128)] for h in range(GROUP)], axis=0)
        keys = kk[pl.ds(1024 * i, 1024), :]
        scores = lax.dot_general(queries, keys, contract, preferred_element_type=jnp.float32)
        fresh = lax.dot_general(queries, nk[top_rows, :], contract, preferred_element_type=jnp.float32)
        scores = scores.reshape(8, 2, 8, 1024)
        fresh = fresh.reshape(8, 2, 8, 16)
        halves = []
        for t in range(2):
            base = 16 * i + 8 * t
            count = spread(lambda r: lens[r], base)[:, :1]
            valid = (lane_wide // CACHE == sub_wide) & (lane_wide % CACHE < count)
            mine = lane_new == sub_new + 8 * t
            s = jnp.where(valid[None], scores[:, t, :, 512 * t : 512 * t + 512] * scale, NEG)
            f = jnp.where(mine[None], fresh[:, t] * scale, NEG)
            top = jnp.maximum(jnp.max(s, axis=2, keepdims=True), jnp.max(f, axis=2, keepdims=True))
            es, ef = jnp.exp(s - top), jnp.exp(f - top)
            total = jnp.sum(es, axis=2, keepdims=True) + jnp.sum(ef, axis=2, keepdims=True)
            inv = 1.0 / total
            ws_ = (es * inv).reshape(64, 512).astype(jnp.bfloat16)
            wf = (ef * inv).reshape(64, 16).astype(jnp.bfloat16)
            o = jnp.dot(ws_, vv[pl.ds(1024 * i + 512 * t, 512), :], preferred_element_type=jnp.float32)
            o = o + jnp.dot(wf, nv[top_rows, :], preferred_element_type=jnp.float32)
            halves.append(o)
        for h in range(GROUP):
            block = jnp.concatenate([o[8 * h : 8 * h + 8] for o in halves], axis=0)
            att[top_rows, pl.ds(128 * h, 128)] = block.astype(jnp.bfloat16)

    lane = lax.broadcasted_iota(jnp.int32, (8, 128), 1)
    lane_group = lane // RANK

    def place_rows():
        named = [spread(lambda r: ad[r], 8 * i) for i in range(8)]
        slot = jnp.concatenate([spread(lambda r: home[ad[r]], 8 * i) for i in range(8)], axis=0)
        named = jnp.concatenate(named, axis=0)
        row_lane = lax.broadcasted_iota(jnp.int32, (ROWS, 128), 1)
        hot = jnp.where(named == row_lane, 1.0, 0.0).astype(jnp.bfloat16)
        same = lax.dot_general(hot, hot, contract, preferred_element_type=jnp.float32)
        before = lax.broadcasted_iota(jnp.int32, (ROWS, ROWS), 1) < lax.broadcasted_iota(
            jnp.int32, (ROWS, ROWS), 0
        )
        twin = jnp.sum(jnp.where(before, same, 0.0), axis=1, keepdims=True) > 0.5
        c, xx, yy = (slot // 2) % 2, (slot // 4) % 4, slot // 16
        a, b = jnp.where(c == 0, xx, yy), jnp.where(c == 0, yy, xx)
        place = (((c * 4 + b) * 4 + a) * 2 + slot % 2) * 2 + twin.astype(jnp.int32)
        return jnp.where(place == row_lane, 1.0, 0.0).astype(jnp.bfloat16)

    def project(first, last):
        for t in range(first, last):
            ws[t].wait()

        def step(t, carry):
            part[t] = jnp.dot(att[...], w[t], preferred_element_type=jnp.float32)
            return carry

        lax.fori_loop(first, last, step, 0)

    def along(d):
        return (req, (z + d) % 8)

    def sum_copy(j, way, d):
        return send(rs_src.at[j, way], rs_dst.at[j, way], rs_send.at[j, way], rs_recv.at[j, way], along(d))

    def first_sums():
        far = []
        for way, d in enumerate((2, 6)):
            cols = pl.ds(256 * way, 256)
            rs_src[0, way, :, cols] = part[0, :, cols].astype(jnp.bfloat16)
            far.append(
                send(
                    rs_src.at[0, way, :, cols], rs_dst.at[0, way, :, cols], rs_send.at[0, way], rs_recv.at[0, way],
                    along(d),
                )
            )
        for way, d in enumerate((1, 7)):
            rs_src[1, way] = part[1 + way].astype(jnp.bfloat16)
            far.append(sum_copy(1, way, d))
        return far

    def near_sums():
        near = []
        for way, d in enumerate((1, 7)):
            rs_src[2, way] = part[3 + way].astype(jnp.bfloat16)
            near.append(sum_copy(2, way, d))
        return near

    def second_sums(far):
        for copy in far:
            copy.wait_recv()
        last = []
        for way, d in enumerate((2, 6)):
            for half in range(2):
                cols = pl.ds(256 * half, 256)
                value = part[5 + way, :, cols] + rs_dst[1, way, :, cols].astype(jnp.float32)
                if half == way:
                    value = value + rs_dst[0, way, :, cols].astype(jnp.float32)
                rs_src[3, way, :, cols] = value.astype(jnp.bfloat16)
            last.append(sum_copy(3, way, d))
        return last

    for i in (0, 3, 4, 5):
        loads[i].wait()
    for c in kv[:4]:
        c.wait()
    attend(0)
    attend(1)
    pl.semaphore_wait(barrier, len(peers))

    loads[6].wait()
    loads[7].wait()
    pools = []
    for p, pool in enumerate((pool_d, pool_u)):
        for j, d in enumerate((2, 1, 3)):
            ref = pool.at[own_rows]
            pools.append(send(ref, ref, pool_send.at[p, j], pool_recv.at[p, j], peer_a(d)))
    for c in ws:
        c.start()

    for i in (1, 2):
        loads[i].wait()
    for c in kv[4:]:
        c.wait()
    place = place_rows()
    attend(2)
    attend(3)

    moved = lax.dot_general(place, att[...], (((0,), (0,)), ((), ())), preferred_element_type=jnp.float32)
    x_src[...] = moved.astype(jnp.bfloat16).reshape(8, 16, 1024)
    for kind in range(2):
        j = y if kind == 0 else x
        for d in (2, 1, 3):
            send(
                x_src.at[kind * 4 + (j + d) % 4], x_dst.at[core * 4 + j],
                x_send.at[kind * 3 + d - 1], x_recv.at[core * 3 + d - 1], owner(kind, d),
            )
    send(
        x_src.at[sib_bundle], x_dst.at[core * 4 + jnp.where(core == 0, x, y)], x_send.at[6], x_recv.at[6], sibling
    )
    x_dst[own_bundle] = x_src[own_bundle]

    project(0, 5)
    far = first_sums()

    for copy in pools[:3]:
        copy.wait_recv()
    for c in range(2):
        for d in range(1, 4):
            here = c * 4 + (b_me - d + 4) % 4
            received(x_src.at[0], x_dst.at[here], x_recv.at[c * 3 + d - 1])
    received(x_src.at[0], x_dst.at[sib_source], x_recv.at[6])

    inner = lax.dot_general(
        x_dst[...].reshape(128, 1024), pool_d[...], contract, preferred_element_type=jnp.float32
    )
    tall = lax.broadcasted_iota(jnp.int32, (128, 128), 0)
    wide_group = lax.broadcasted_iota(jnp.int32, (128, 128), 1) // RANK
    mine = wide_group == (tall % 16) // 2

    def fold(value):
        for shift in (64, 32, 16):
            value = value + pltpu.roll(value, shift, 1)
        return value

    inner = fold(jnp.where(mine, inner, 0.0))
    halves = []
    for half in range(2):
        packed = jnp.zeros((8, 128), jnp.float32)
        for i in range(8):
            row = 64 * half + 8 * i
            packed = jnp.where(lane_group == i, inner[row : row + 8], packed)
        halves.append(packed)
    low_own[...] = jnp.concatenate(halves, axis=0).astype(jnp.bfloat16)
    low_all[z] = low_own[...]
    for d in (4, 3, 5, 2, 6, 1, 7):
        send(low_own, low_all.at[z], low_send.at[d - 1], low_recv.at[d - 1], (req, (z + d) % 8))

    near = near_sums()
    project(5, 8)
    last = second_sums(far)

    for d in range(1, 8):
        received(low_own, low_all.at[(z - d + 8) % 8], low_recv.at[d - 1])
    total = low_all[0].astype(jnp.float32)
    for j in range(1, 8):
        total = total + low_all[j].astype(jnp.float32)
    rows = [jnp.where(lane_group == i % 8, total[i // 8 * 8 : i // 8 * 8 + 8], 0.0) for i in range(16)]
    for copy in pools[3:]:
        copy.wait_recv()
    low = jnp.where(mine, fold(jnp.concatenate(rows, axis=0)), 0.0).astype(jnp.bfloat16)
    delta = jnp.dot(low, pool_u[...], preferred_element_type=jnp.float32)
    y_src[...] = delta.astype(jnp.bfloat16).reshape(8, 16, 512)

    earlier = len(started)
    for c in range(2):
        for d in (2, 1, 3):
            send(
                y_src.at[c * 4 + (b_me + d) % 4], y_dst.at[own_bundle],
                y_send.at[c * 3 + d - 1], y_recv.at[core * 3 + d - 1], source(c, d),
            )
    send(y_src.at[sib_source], y_dst.at[own_bundle], y_send.at[6], y_recv.at[6], sibling)
    y_dst[own_bundle] = y_src[own_bundle]

    for j, copies in ((2, near), (3, last)):
        for way, copy in enumerate(copies):
            copy.wait_recv()
            part[7] = part[7] + rs_dst[j, way].astype(jnp.float32)
    for copy in started[:earlier]:
        copy.wait_send()

    for kind in range(2):
        j = y if kind == 0 else x
        for d in range(1, 4):
            received(y_src.at[0], y_dst.at[kind * 4 + (j - d + 4) % 4], y_recv.at[kind * 3 + d - 1])
    received(y_src.at[0], y_dst.at[sib_bundle], y_recv.at[6])
    change = jnp.dot(place, y_dst[...].reshape(128, 512), preferred_element_type=jnp.float32)
    out_ref[...] = (part[7] + change).astype(jnp.bfloat16)
    for copy in started[earlier:]:
        copy.wait_send()


def per_device(
    queries, key_cache, value_cache, new_key, new_value, cache_length, row_adapter, adapter_home,
    down_pool, up_pool, out_weight,
):
    down = jnp.transpose(down_pool, (0, 2, 1)).reshape(32, 1024)
    up = up_pool.reshape(32, 512)
    keys = key_cache.reshape(4096, 128)
    values = value_cache.reshape(4096, 128)
    named = row_adapter.reshape(64)
    hbm = pl.BlockSpec(memory_space=pltpu.HBM)
    bf16 = jnp.bfloat16
    dma, vmem, smem = pltpu.SemaphoreType.DMA, pltpu.VMEM, pltpu.SMEM
    return pl.pallas_call(
        kernel,
        out_shape=jax.ShapeDtypeStruct((64, 512), bf16),
        in_specs=[hbm] * 11,
        out_specs=pl.BlockSpec(memory_space=pltpu.VMEM),
        scratch_shapes=[
            vmem((64, 1024), bf16),
            vmem((4096, 128), bf16),
            vmem((4096, 128), bf16),
            vmem((64, 128), bf16),
            vmem((64, 128), bf16),
            smem((64,), jnp.int32),
            smem((64,), jnp.int32),
            smem((64,), jnp.int32),
            vmem((128, 1024), bf16),
            vmem((128, 512), bf16),
            vmem((8, 1024, 512), bf16),
            vmem((64, 1024), bf16),
            vmem((8, 64, 512), jnp.float32),
            vmem((4, 2, 64, 512), bf16),
            vmem((4, 2, 64, 512), bf16),
            vmem((8, 16, 1024), bf16),
            vmem((8, 16, 1024), bf16),
            vmem((16, 128), bf16),
            vmem((8, 16, 128), bf16),
            vmem((8, 16, 512), bf16),
            vmem((8, 16, 512), bf16),
            dma((8,)),
            dma((2, 4)),
            dma((8,)),
            dma((2, 3)),
            dma((2, 3)),
            dma((7,)),
            dma((7,)),
            dma((7,)),
            dma((7,)),
            dma((7,)),
            dma((7,)),
            dma((4, 2)),
            dma((4, 2)),
        ],
        compiler_params=pltpu.CompilerParams(
            collective_id=0, has_side_effects=True, vmem_limit_bytes=60 * 1024 * 1024
        ),
    )(
        queries, keys, values, new_key, new_value, cache_length, named, adapter_home, down, up, out_weight
    )


def solution(mesh):
    return jax.shard_map(
        per_device,
        mesh=mesh,
        in_specs=(
            P("req", "tp"),
            P("req", "tp", None, None),
            P("req", "tp", None, None),
            P("req", "tp"),
            P("req", "tp"),
            P("req"),
            P("req", None),
            P(),
            P("req", "tp", None),
            P("req", None, "tp"),
            P("tp", None),
        ),
        out_specs=P("req", "tp"),
        check_vma=False,
    )
```
